512 devices in a mesh: ctx: 16 (over y, x), head: 32 (over z, core).
Axes of the slice: x: 4, y: 4, z: 16, core: 2. Of those that a mesh axis runs over, the one named last changes fastest.
Arguments:
- queries: bfloat16 [32, 96, 65536], P(None, None, ('ctx', 'head')), may hold values from -9 to 9
- keys: bfloat16 [32, 96, 65536], P(None, None, ('ctx', 'head')), may hold values from -9 to 9
- values: bfloat16 [32, 96, 65536], P(None, None, ('ctx', 'head')), may hold values from -6 to 6
- doc_start: int32 [65536], P(('ctx', 'head')), may hold values from 0 to 65535, as said below
Outputs:
- grad_queries: bfloat16 [32, 96, 65536], P(None, None, ('ctx', 'head'))
- grad_keys: bfloat16 [32, 96, 65536], P(None, None, ('ctx', 'head'))
- grad_values: bfloat16 [32, 96, 65536], P(None, None, ('ctx', 'head'))
The draws below stay inside these ranges and needn't reach their ends.
Inputs may be any that keep to these rules, and one draw needn't show every extreme that they name: doc_start never falls; doc_start[t] is t or doc_start[t-1], t - doc_start[t] < 512, the first document has exactly 512 positions, and at every multiple k of 4096 after 0 a document starts at k - 256 and runs through k + 512 // 2 - 1.
All inputs are finite; a program needn't handle non-finite values.
Results may differ from the reference program's by a relative error of at most 0.02.
Values may be sent and summed in bfloat16 or wider, within the bound.
No kernel may reach another device: no remote copies, remote signals or barrier semaphores. Data moves between devices by JAX's collectives and lax.ppermute only.
A program may use at most 128 MiB of HBM per device.

```python
import math
import jax
import jax.numpy as jnp
from jax import lax

HEADS = 32
HEAD_DIM = 96
TOK_DEV = 128
DOC_MAX = 512
TOKENS = 65536
N_HEAD = 32


def draw_queries(key, part):
    key = jax.random.fold_in(key, 3)
    planted = jnp.clip(jax.random.normal(key, (HEADS, HEAD_DIM, TOKENS)), -5.0, 5.0)
    return planted.astype(jnp.bfloat16)


def draw_keys(key, part):
    key = jax.random.fold_in(key, 5)
    planted = jnp.clip(jax.random.normal(key, (HEADS, HEAD_DIM, TOKENS)), -5.0, 5.0)
    return planted.astype(jnp.bfloat16)


def draw_doc_start(key, part):
    key = jax.random.fold_in(key, 7)
    rolls = jax.random.randint(key, (TOKENS,), 0, max(DOC_MAX // 4, 2))
    positions = jnp.arange(TOKENS, dtype=jnp.int32)
    group_span = TOK_DEV * N_HEAD
    half_doc = DOC_MAX // 2

    def advance(current, pair):
        position, roll = pair
        phase = position % group_span
        planted = (phase == group_span - half_doc) & (position >= DOC_MAX)
        banned = (phase > group_span - half_doc) | (phase < half_doc)
        chosen = (position >= DOC_MAX) & (roll == 0) & jnp.logical_not(banned)
        fresh = (position == 0) | planted | chosen | (position - current >= DOC_MAX)
        current = jnp.where(fresh, position, current)
        return (current, current)
    _, starts = lax.scan(advance, jnp.int32(0), (positions, rolls))
    return starts


def block_levels(own_key, dims, shards, smallest, top_value):
    gain, own = 1.0, jax.random.fold_in(own_key, 6)
    for dim, shards_of in shards:
        heights = jnp.exp(jax.random.uniform(jax.random.fold_in(own, dim), (shards_of,), jnp.float32, smallest / len(shards), top_value / len(shards)))
        gain = gain * jnp.repeat(heights, dims[dim] // shards_of).reshape([-1 if axis == dim else 1 for axis in range(len(dims))])
    return gain


def scatter_about(key, shape, deviation, reach, pieces=(), held_as=jnp.bfloat16):
    drawn = deviation * jax.random.normal(key, shape, jnp.float32)
    if pieces:
        drawn = drawn * block_levels(key, shape, pieces, -0.22, 0.18)
    return jnp.clip(drawn, -reach, reach).astype(held_as)


def setup_inputs(seed: int = 0) -> dict:
    arg_keys = jax.random.split(jax.random.key(seed), 5)
    return {
        "queries": draw_queries(jax.random.fold_in(arg_keys[4], 71), 0),
        "keys": draw_keys(jax.random.fold_in(arg_keys[4], 71), 0),
        "values": scatter_about(arg_keys[2], (HEADS, HEAD_DIM, TOKENS), 1.0, 6.0, ((2, 512),)),
        "doc_start": draw_doc_start(jax.random.fold_in(arg_keys[4], 71), 0),
    }


def block_grads(query_blk, key_win, value_win, first_pos, query_pos, key_pos, score_scale):
    visible = (key_pos[None, :] >= first_pos[:, None]) & (key_pos[None, :] <= query_pos[:, None])
    query_wide = query_blk.astype(jnp.float32)
    key_wide = key_win.astype(jnp.float32)
    value_wide = value_win.astype(jnp.float32)
    scores = jnp.einsum('hdq,hdk->hqk', query_wide, key_wide) * score_scale
    scores = jnp.where(visible[None], scores, -jnp.inf)
    row_peak = lax.optimization_barrier(jnp.max(scores, axis=2, keepdims=True))
    weights = jnp.exp(scores - row_peak)
    soft_probs = weights / lax.optimization_barrier(jnp.sum(weights, axis=2, keepdims=True))
    probs_low = lax.optimization_barrier(soft_probs.astype(jnp.bfloat16)).astype(jnp.float32)
    attended = jnp.einsum('hqk,hdk->hdq', probs_low, value_wide).astype(jnp.bfloat16)
    attended = lax.optimization_barrier(attended).astype(jnp.float32)
    grad_value = jnp.einsum('hqk,hdq->hdk', probs_low, attended)
    grad_probs = jnp.einsum('hdq,hdk->hqk', attended, value_wide)
    row_dot = lax.optimization_barrier(jnp.sum(attended * attended, axis=1))
    grad_scores = (soft_probs * (grad_probs - row_dot[:, :, None])).astype(jnp.bfloat16)
    grad_scores = lax.optimization_barrier(grad_scores).astype(jnp.float32)
    grad_query = (jnp.einsum('hqk,hdk->hdq', grad_scores, key_wide) * score_scale).astype(jnp.bfloat16)
    grad_key = jnp.einsum('hqk,hdq->hdk', grad_scores, query_wide)
    return (grad_query, grad_key, grad_value)

def reference(queries, keys, values, doc_start):
    head_count, head_depth, total = queries.shape
    score_scale = 1.0 / math.sqrt(head_depth)
    window = DOC_MAX
    blocks = total // window
    padding = jnp.zeros((head_count, head_depth, window), queries.dtype)
    key_ext = jnp.concatenate([padding, keys], axis=2)
    value_ext = jnp.concatenate([padding, values], axis=2)
    offsets = jnp.arange(window, dtype=jnp.int32)
    spread = jnp.arange(2 * window, dtype=jnp.int32)

    def one_block(near_prev, number):
        block_base = (number * window).astype(jnp.int32)
        query_blk = lax.dynamic_slice_in_dim(queries, block_base, window, 2)
        key_win = lax.dynamic_slice_in_dim(key_ext, block_base, 2 * window, 2)
        value_win = lax.dynamic_slice_in_dim(value_ext, block_base, 2 * window, 2)
        first_pos = lax.dynamic_slice_in_dim(doc_start, block_base, window, 0)
        query_pos = block_base + offsets
        key_pos = block_base - window + spread
        grad_query, grad_key, grad_value = block_grads(query_blk, key_win, value_win, first_pos, query_pos, key_pos, score_scale)
        done_key = ((near_prev[0] + grad_key[:, :, :window]) * score_scale).astype(jnp.bfloat16)
        done_value = (near_prev[1] + grad_value[:, :, :window]).astype(jnp.bfloat16)
        return ((grad_key[:, :, window:], grad_value[:, :, window:]), (grad_query, done_key, done_value))
    start_carry = (jnp.zeros((head_count, head_depth, window), jnp.float32), jnp.zeros((head_count, head_depth, window), jnp.float32))
    last_carry, (query_stack, key_stack, value_stack) = lax.scan(one_block, start_carry, jnp.arange(blocks, dtype=jnp.int32))
    last_key = (last_carry[0] * score_scale).astype(jnp.bfloat16)
    last_value = last_carry[1].astype(jnp.bfloat16)
    key_stack = jnp.concatenate([key_stack[1:], last_key[None]], axis=0)
    value_stack = jnp.concatenate([value_stack[1:], last_value[None]], axis=0)

    def to_whole(stacked):
        return jnp.moveaxis(stacked, 0, 2).reshape(head_count, head_depth, total)
    return (to_whole(query_stack), to_whole(key_stack), to_whole(value_stack))
```

```python
import functools
import math

import jax
import jax.numpy as jnp
from jax import lax
from jax.experimental import pallas as pl
from jax.experimental.pallas import tpu as pltpu
from jax.sharding import PartitionSpec as P

CHUNKS = (4, 4, 4, 4)
LOG2E = 1.4426950408889634
HIDDEN = -1e30


def dot_tn(a, b):
    return lax.dot_general(a, b, (((0,), (0,)), ((), ())), preferred_element_type=jnp.float32)


def dot_nt(a, b):
    return lax.dot_general(a, b, (((1,), (1,)), ((), ())), preferred_element_type=jnp.float32)


def dot_nn(a, b):
    return lax.dot_general(a, b, (((1,), (0,)), ((), ())), preferred_element_type=jnp.float32)


def attention_kernel(
    first_ref, lo_ref, q_ref, kv0_ref, kv1_ref, kv2_ref, dq_ref, d0_ref, d1_ref, d2_ref, *, score_scale
):
    heads = q_ref.shape[1]
    half = q_ref.shape[3]
    span = 2 * half
    lo = lo_ref[...]
    refs = (kv2_ref, kv1_ref, kv0_ref)
    outs = (d2_ref, d1_ref, d0_ref)

    def wide(ref, *index):
        return jnp.concatenate([ref[(0, *index)], ref[(1, *index)]], axis=1)

    def put(ref, index, value):
        ref[(0, *index)] = value[:, :half].astype(ref.dtype)
        ref[(1, *index)] = value[:, half:].astype(ref.dtype)

    def run(first_block):
        number = range(first_block, 3)
        for h in range(heads):
            q = wide(q_ref, h)
            scores = {}
            for b in number:
                raw = dot_tn(wide(refs[b], h, 0), q) * (score_scale * LOG2E)
                key_pos = lax.broadcasted_iota(jnp.int32, (span, span), 0) + b * span
                visible = key_pos >= lo
                if b == 2:
                    row = lax.broadcasted_iota(jnp.int32, (span, span), 1) + b * span
                    visible = visible & (key_pos <= row)
                scores[b] = jnp.where(visible, raw, HIDDEN)
            peak = functools.reduce(
                jnp.maximum, [jnp.max(scores[b], axis=0, keepdims=True) for b in number]
            )
            weights = {b: jnp.exp2(scores[b] - peak) for b in number}
            total = sum(jnp.sum(weights[b], axis=0, keepdims=True) for b in number)
            inverse = 1.0 / total
            probs = {b: weights[b] * inverse for b in number}
            low = {b: probs[b].astype(jnp.bfloat16) for b in number}
            attended = sum(dot_nn(wide(refs[b], h, 1), low[b]) for b in number).astype(jnp.bfloat16)
            wide_att = attended.astype(jnp.float32)
            row_dot = jnp.sum(wide_att * wide_att, axis=0, keepdims=True)
            dq = jnp.zeros((q.shape[0], span), jnp.float32)
            for b in number:
                put(outs[b], (h, 1), dot_nt(attended, low[b]))
                grad_probs = dot_tn(wide(refs[b], h, 1), attended)
                grad_scores = (probs[b] * (grad_probs - row_dot)).astype(jnp.bfloat16)
                dq = dq + dot_nn(wide(refs[b], h, 0), grad_scores)
                put(outs[b], (h, 0), dot_nt(q, grad_scores) * score_scale)
            put(dq_ref, (h,), dq * score_scale)
        for b in range(first_block):
            outs[b][...] = jnp.zeros_like(outs[b])

    far = first_ref[0] < span

    @pl.when(far)
    def _():
        run(0)

    @pl.when(jnp.logical_not(far))
    def _():
        run(1)


def attention(first, lo, q, kv0, kv1, kv2, chunk_start, score_scale, per_step):
    _, chunk, _, depth, half = kv0.shape
    q_spec = pl.BlockSpec((2, per_step, depth, half), lambda g, s: (0, g + chunk_start // per_step, 0, 0))
    dq_spec = pl.BlockSpec((2, per_step, depth, half), lambda g, s: (0, g, 0, 0))
    kv_spec = pl.BlockSpec((2, per_step, 2, depth, half), lambda g, s: (0, g, 0, 0, 0))
    lo_spec = pl.BlockSpec((1, 2 * half), lambda g, s: (0, 0))
    kv_shape = (2, chunk, 2, depth, half)
    pairs = chunk * (2 * half) * (6 * half)
    return pl.pallas_call(
        functools.partial(attention_kernel, score_scale=score_scale),
        grid_spec=pltpu.PrefetchScalarGridSpec(
            num_scalar_prefetch=1,
            grid=(chunk // per_step,),
            in_specs=[lo_spec, q_spec, kv_spec, kv_spec, kv_spec],
            out_specs=[dq_spec, kv_spec, kv_spec, kv_spec],
        ),
        out_shape=[
            jax.ShapeDtypeStruct((2, chunk, depth, half), jnp.bfloat16),
            jax.ShapeDtypeStruct(kv_shape, jnp.float32),
            jax.ShapeDtypeStruct(kv_shape, jnp.bfloat16),
            jax.ShapeDtypeStruct(kv_shape, jnp.bfloat16),
        ],
        compiler_params=pltpu.CompilerParams(vmem_limit_bytes=32 * 1024 * 1024),
        cost_estimate=pl.CostEstimate(
            flops=pairs * depth * 12, bytes_accessed=chunk * depth * half * 40, transcendentals=pairs
        ),
        name="attention",
    )(first, lo, q, kv0, kv1, kv2)


def shards(queries, keys, values, doc_start):
    heads, depth, half = queries.shape
    score_scale = 1.0 / math.sqrt(depth)
    ctx_count = lax.axis_size("ctx")
    head_count = lax.axis_size("head")
    chips = head_count // 2
    mine = heads // 2
    span = 2 * half
    pairs = [[2 * z, 2 * z + 1] for z in range(chips)]

    def cores(value):
        return lax.all_to_all(
            value, "head", split_axis=0, concat_axis=0, tiled=True, axis_index_groups=pairs
        )

    count = ctx_count * head_count
    near_up = [(s, s + 2) for s in range(count - 2)]
    near_down = [(s + 2, s) for s in range(count - 2)]
    far_up = [(s, s + 2) for s in range(2, head_count - 2)]
    far_down = [(s + 2, s) for s in range(2, head_count - 2)]
    flat = ("ctx", "head")

    other = lax.ppermute(doc_start, "head", [(s, s ^ 1) for s in range(head_count)])
    place = lax.axis_index("head")
    odd = place % 2
    starts = jnp.where(
        odd == 0, jnp.concatenate([doc_start, other]), jnp.concatenate([other, doc_start])
    )
    base = (lax.axis_index("ctx") * chips + place // 2) * span
    lo = (starts - (base - 2 * span)).reshape(1, span)
    first = lo[0, :1]

    packed = jnp.stack(
        [keys.reshape(2, mine, depth, half), values.reshape(2, mine, depth, half)], axis=2
    )
    packed = cores(packed)
    q_all = cores(queries.reshape(2, mine, depth, half))

    dq_parts, dkv_parts = [], []
    begin = 0
    for chunk in CHUNKS:
        kv0 = packed[:, begin : begin + chunk]
        kv1 = lax.ppermute(kv0, flat, near_up)
        kv2 = lax.ppermute(kv1, "head", far_up)
        dq, d0, d1, d2 = attention(first, lo, q_all, kv0, kv1, kv2, begin, score_scale, 2)
        back2 = lax.ppermute(d2, "head", far_down)
        d1 = (d1.astype(jnp.float32) + back2.astype(jnp.float32)).astype(jnp.bfloat16)
        back1 = lax.ppermute(d1, flat, near_down)
        dq_parts.append(dq)
        dkv_parts.append((d0 + back1.astype(jnp.float32)).astype(jnp.bfloat16))
        begin += chunk

    def home(value):
        return cores(value).reshape(heads, depth, half)

    dkv = jnp.concatenate(dkv_parts, axis=1)
    return (
        home(jnp.concatenate(dq_parts, axis=1)),
        home(dkv[:, :, 0]),
        home(dkv[:, :, 1]),
    )


def solution(mesh):
    return jax.shard_map(
        shards,
        mesh=mesh,
        in_specs=(
            P(None, None, ("ctx", "head")),
            P(None, None, ("ctx", "head")),
            P(None, None, ("ctx", "head")),
            P(("ctx", "head")),
        ),
        out_specs=(
            P(None, None, ("ctx", "head")),
            P(None, None, ("ctx", "head")),
            P(None, None, ("ctx", "head")),
        ),
        check_vma=False,
    )
```

```python
import functools
import math

import jax
import jax.numpy as jnp
from jax import lax
from jax.experimental import pallas as pl
from jax.experimental.pallas import tpu as pltpu
from jax.sharding import PartitionSpec as P

CHUNKS = (8, 8)
PER_STEP = 4
GROUP = 4
MARK_ROWS = 16
VMEM = 32 * 1024 * 1024
LOG2E = 1.4426950408889634
HIDDEN = -1e30


def dot_tn(a, b):
    return lax.dot_general(a, b, (((0,), (0,)), ((), ())), preferred_element_type=jnp.float32)


def dot_nt(a, b):
    return lax.dot_general(a, b, (((1,), (1,)), ((), ())), preferred_element_type=jnp.float32)


def dot_nn(a, b):
    return lax.dot_general(a, b, (((1,), (0,)), ((), ())), preferred_element_type=jnp.float32)


def pack_kernel(first_ref, start_ref, k_ref, v_ref, q_ref, out_ref):
    _, chunk, depth, half = k_ref.shape
    into = first_ref[0] + lax.broadcasted_iota(jnp.int32, (1, half), 1) - start_ref[...]
    row = lax.broadcasted_iota(jnp.int32, (MARK_ROWS, half), 0)
    coarse, fine = into // 2, into % 2
    marks = jnp.where(row == 0, coarse, jnp.where(row == 1, fine, 0))
    marks = marks.astype(jnp.float32).astype(jnp.bfloat16)
    for core in range(2):
        for h in range(chunk):
            for n, ref in enumerate((k_ref, v_ref, q_ref)):
                out_ref[core, pl.ds((3 * h + n) * depth, depth), :] = ref[core, h]
        out_ref[core, pl.ds(3 * chunk * depth, MARK_ROWS), :] = marks


def pack(first, starts, keys, values, queries, begin, chunk):
    _, _, depth, half = keys.shape
    block = pl.BlockSpec((2, chunk, depth, half), lambda g, s: (0, begin // chunk, 0, 0))
    shape = (2, 3 * chunk * depth + MARK_ROWS, half)
    return pl.pallas_call(
        pack_kernel,
        grid_spec=pltpu.PrefetchScalarGridSpec(
            num_scalar_prefetch=1,
            grid=(1,),
            in_specs=[pl.BlockSpec((1, half), lambda g, s: (0, 0)), block, block, block],
            out_specs=pl.BlockSpec(shape, lambda g, s: (0, 0, 0)),
        ),
        out_shape=jax.ShapeDtypeStruct(shape, jnp.bfloat16),
        compiler_params=pltpu.CompilerParams(vmem_limit_bytes=VMEM),
        name="pack",
    )(first, starts, keys, values, queries)


def attention_kernel(
    edge_ref,
    marks_next_ref,
    marks_own_ref,
    next0_ref,
    next1_ref,
    own0_ref,
    own1_ref,
    prior_ref,
    to_next_ref,
    kept_ref,
    to_prior_ref,
    *,
    score_scale,
):
    _, heads, _, depth, half = to_prior_ref.shape
    span = 2 * half
    place = lax.broadcasted_iota(jnp.int32, (1, span), 1)
    prior, own, following = range(3)
    outs = (to_prior_ref, kept_ref, to_next_ref)

    def first_visible(marks_ref, before):
        marks = jnp.concatenate([marks_ref[0], marks_ref[1]], axis=1).astype(jnp.float32)
        into = (marks[0:1] * 2 + marks[1:2]).astype(jnp.int32)
        return before * span + place - into

    def load(b, h, n):
        if b == prior:
            return jnp.concatenate([prior_ref[0, h, n], prior_ref[1, h, n]], axis=1)
        first, second = ((own0_ref, own1_ref), (next0_ref, next1_ref))[b - 1]
        rows = pl.ds((3 * h + n) * depth, depth)
        return jnp.concatenate([first[0, rows, :], second[0, rows, :]], axis=1)

    def put(ref, index, value, add):
        for core in range(2):
            part = value[:, core * half : (core + 1) * half]
            if add:
                part = part + ref[(core, *index)].astype(jnp.float32)
            ref[(core, *index)] = part.astype(ref.dtype)

    def run(blocks, lo, rows_ref, add=None):
        diagonal = len(blocks) - 1
        hidden = []
        for at in range(len(blocks)):
            key_pos = lax.broadcasted_iota(jnp.int32, (span, span), 0) + at * span
            visible = key_pos >= lo
            if at == diagonal:
                row = lax.broadcasted_iota(jnp.int32, (span, span), 1) + at * span
                visible = visible & (key_pos <= row)
            hidden.append(jnp.where(visible, 0.0, HIDDEN))
        ones = jnp.ones((MARK_ROWS, span), jnp.bfloat16)
        for begin in range(0, heads, GROUP):
            group = range(begin, begin + GROUP)
            keys = {h: [load(b, h, 0) for b in blocks] for h in group}
            values = {h: [load(b, h, 1) for b in blocks] for h in group}
            q = {h: load(blocks[-1], h, 2) for h in group}
            scores = {
                h: [
                    dot_tn(key, q[h]) * (score_scale * LOG2E) + mask
                    for key, mask in zip(keys[h], hidden)
                ]
                for h in group
            }
            peak = {
                h: functools.reduce(
                    jnp.maximum, [jnp.max(score, axis=0, keepdims=True) for score in scores[h]]
                )
                for h in group
            }
            wide = {h: [jnp.exp2(score - peak[h]) for score in scores[h]] for h in group}
            low = {h: [weight.astype(jnp.bfloat16) for weight in wide[h]] for h in group}
            raw = {
                h: sum(
                    dot_nn(jnp.concatenate([value, ones], axis=0), weight)
                    for value, weight in zip(values[h], low[h])
                )
                for h in group
            }
            shared, row_dot = {}, {}
            for h in group:
                inverse = 1.0 / raw[h][depth : depth + 1]
                attended = (raw[h][:depth] * inverse).astype(jnp.bfloat16).astype(jnp.float32)
                row_dot[h] = jnp.sum(attended * attended, axis=0, keepdims=True) * inverse
                shared[h] = (attended * inverse).astype(jnp.bfloat16)
            grad_values = {h: [dot_nt(shared[h], weight) for weight in low[h]] for h in group}
            grad_scores = {
                h: [
                    (weight * (dot_tn(value, shared[h]) - row_dot[h])).astype(jnp.bfloat16)
                    for value, weight in zip(values[h], wide[h])
                ]
                for h in group
            }
            dq = {
                h: sum(dot_nn(key, grad) for key, grad in zip(keys[h], grad_scores[h]))
                for h in group
            }
            grad_keys = {h: [dot_nt(q[h], grad) for grad in grad_scores[h]] for h in group}
            for h in group:
                for at, b in enumerate(blocks):
                    put(outs[b], (h, 1), grad_values[h][at], b == add)
                    put(outs[b], (h, 0), grad_keys[h][at] * score_scale, b == add)
                put(rows_ref, (h, 2), dq[h] * score_scale, False)

    def clear(ref, kinds):
        for n in kinds:
            ref[:, :, n] = jnp.zeros_like(ref[:, :, n])

    edge = edge_ref[0] == 1

    @pl.when(jnp.logical_not(edge))
    def _():
        lo = first_visible(marks_next_ref, 2)
        far = jnp.min(lo) < span
        clear(kept_ref, (2,))

        @pl.when(far)
        def _():
            run((prior, own, following), lo, to_next_ref)

        @pl.when(jnp.logical_not(far))
        def _():
            run((own, following), lo - span, to_next_ref)
            clear(to_prior_ref, (0, 1))

    @pl.when(edge)
    def _():
        lo_own = first_visible(marks_own_ref, 1)
        lo_next = first_visible(marks_next_ref, 1)
        across_own = jnp.min(lo_own) < span
        across_next = jnp.min(lo_next) < span

        @pl.when(across_own)
        def _():
            run((prior, own), lo_own, kept_ref)

        @pl.when(jnp.logical_not(across_own))
        def _():
            run((own,), lo_own - span, kept_ref)
            clear(to_prior_ref, (0, 1))

        @pl.when(across_next)
        def _():
            run((own, following), lo_next, to_next_ref, add=own)

        @pl.when(jnp.logical_not(across_next))
        def _():
            run((following,), lo_next - span, to_next_ref)


def attention(edge, following, own, prior, score_scale):
    _, chunk, _, depth, half = prior.shape
    rows = 3 * PER_STEP * depth

    def spec(kinds):
        return pl.BlockSpec((2, PER_STEP, kinds, depth, half), lambda g, s: (0, g, 0, 0, 0))

    def out(kinds):
        return jax.ShapeDtypeStruct((2, chunk, kinds, depth, half), jnp.bfloat16)

    def side(core):
        return pl.BlockSpec((1, rows, half), lambda g, s: (core, g, 0))

    marks = pl.BlockSpec((2, MARK_ROWS, half), lambda g, s: (0, 3 * chunk * depth // MARK_ROWS, 0))
    pairs = chunk * (2 * half) * (6 * half)
    return pl.pallas_call(
        functools.partial(attention_kernel, score_scale=score_scale),
        grid_spec=pltpu.PrefetchScalarGridSpec(
            num_scalar_prefetch=1,
            grid=(chunk // PER_STEP,),
            in_specs=[marks, marks, side(0), side(1), side(0), side(1), spec(2)],
            out_specs=[spec(3), spec(3), spec(2)],
        ),
        out_shape=[out(3), out(3), out(2)],
        compiler_params=pltpu.CompilerParams(vmem_limit_bytes=VMEM),
        cost_estimate=pl.CostEstimate(
            flops=pairs * depth * 12, bytes_accessed=chunk * depth * half * 40, transcendentals=pairs
        ),
        name="attention",
    )(edge, following, own, following, following, own, own, prior)


def merge_kernel(kept_ref, from_prior_ref, from_next_ref, out_ref):
    for n in range(3):
        total = kept_ref[:, :, n].astype(jnp.float32) + from_prior_ref[:, :, n].astype(jnp.float32)
        if n < 2:
            total = total + from_next_ref[:, :, n].astype(jnp.float32)
        out_ref[:, :, n] = total.astype(jnp.bfloat16)


def merge(kept, from_prior, from_next):
    _, chunk, _, depth, half = kept.shape

    def spec(kinds):
        return pl.BlockSpec((2, PER_STEP, kinds, depth, half), lambda g: (0, g, 0, 0, 0))

    return pl.pallas_call(
        merge_kernel,
        grid=(chunk // PER_STEP,),
        in_specs=[spec(3), spec(3), spec(2)],
        out_specs=spec(3),
        out_shape=jax.ShapeDtypeStruct(kept.shape, jnp.bfloat16),
        compiler_params=pltpu.CompilerParams(vmem_limit_bytes=VMEM),
        name="merge",
    )(kept, from_prior, from_next)


def finish_kernel(early_ref, late_ref, out_q, out_k, out_v, sems):
    begin, mine = early_ref.shape[1], early_ref.shape[1] + late_ref.shape[1]
    pieces = []
    for half in range(2):
        for n, out in enumerate((out_k, out_v, out_q)):
            pieces.append((early_ref.at[half, :, n], out.at[pl.ds(half * mine, begin)]))
            pieces.append((late_ref.at[half, :, n], out.at[pl.ds(half * mine + begin, mine - begin)]))
    copies = [
        pltpu.make_async_copy(source, target, sems.at[i])
        for i, (source, target) in enumerate(pieces)
    ]
    for copy in copies:
        copy.start()
    for copy in copies:
        copy.wait()


def finish(early, late):
    _, begin, _, depth, half = early.shape
    heads = 2 * (begin + late.shape[1])
    out = jax.ShapeDtypeStruct((heads, depth, half), jnp.bfloat16)
    return pl.pallas_call(
        finish_kernel,
        in_specs=[pl.BlockSpec(memory_space=pltpu.VMEM)] * 2,
        out_specs=[pl.BlockSpec(memory_space=pl.ANY)] * 3,
        out_shape=[out] * 3,
        scratch_shapes=[pltpu.SemaphoreType.DMA((12,))],
        compiler_params=pltpu.CompilerParams(vmem_limit_bytes=VMEM),
        name="finish",
    )(early, late)


def after(value, *earlier):
    return lax.optimization_barrier((value, *earlier))[0]


def shards(queries, keys, values, doc_start):
    heads, depth, half = queries.shape
    score_scale = 1.0 / math.sqrt(depth)
    ctx_count = lax.axis_size("ctx")
    head_count = lax.axis_size("head")
    mine = heads // 2
    pairs = [[2 * z, 2 * z + 1] for z in range(head_count // 2)]

    def cores(value):
        return lax.all_to_all(
            value, "head", split_axis=0, concat_axis=0, tiled=True, axis_index_groups=pairs
        )

    column_up = [
        (c * head_count + s, c * head_count + s + 2)
        for c in range(ctx_count)
        for s in range(head_count - 2)
    ]
    across = [
        (c * head_count - 2 + core, c * head_count + core)
        for c in range(1, ctx_count)
        for core in range(2)
    ]
    inner_up = [
        (c * head_count + s, c * head_count + s + 2)
        for c in range(ctx_count)
        for s in range(2, head_count - 4)
    ] + across
    column_down = [(t, s) for s, t in column_up]
    inner_down = [(t, s) for s, t in inner_up]
    flat = ("ctx", "head")
    begins = [sum(CHUNKS[:c]) for c in range(len(CHUNKS) + 1)]
    last = len(CHUNKS) - 1
    by_core = (2, mine, depth, half)
    keys, values, queries = (x.reshape(by_core) for x in (keys, values, queries))
    position = (lax.axis_index("ctx") * head_count + lax.axis_index("head")) * half
    first = position.astype(jnp.int32).reshape(1)
    starts = doc_start.reshape(1, half)

    own, following, prior, to_next, kept, to_prior, back_next, back_prior, done = (
        [None] * len(CHUNKS) for _ in range(9)
    )

    def pair(c):
        body = own[c][:, : 3 * CHUNKS[c] * depth].reshape(2, CHUNKS[c], 3, depth, half)
        return body[:, :, :2]

    for c in range(last + 1):
        packed = pack(first, starts, keys, values, queries, begins[c], CHUNKS[c])
        if c:
            packed = after(packed, own[c - 1])
        own[c] = cores(packed)
        down, up = own[c], pair(c)
        if c:
            down = after(down, following[c - 1])
        following[c] = lax.ppermute(down, flat, column_down)
        prior[c] = lax.ppermute(up, flat, inner_up)

    edge = (lax.axis_index("head") < 2).astype(jnp.int32).reshape(1)
    for c in range(last + 1):
        to_next[c], kept[c], to_prior[c] = attention(
            edge, following[c], own[c], prior[c], score_scale
        )
        back_next[c] = lax.ppermute(
            after(to_next[c], back_next[c - 1] if c else prior[last]), flat, column_up
        )
        back_prior[c] = lax.ppermute(
            after(to_prior[c], back_prior[c - 1] if c else following[last]), flat, inner_down
        )
        done[c] = merge(kept[c], back_next[c], back_prior[c])
    early = cores(done[0] if last == 1 else jnp.concatenate(done[:last], axis=1))
    late = cores(after(done[last], early))
    grad_q, grad_k, grad_v = finish(early, late)
    return grad_q, grad_k, grad_v


def solution(mesh):
    return jax.shard_map(
        shards,
        mesh=mesh,
        in_specs=(
            P(None, None, ("ctx", "head")),
            P(None, None, ("ctx", "head")),
            P(None, None, ("ctx", "head")),
            P(("ctx", "head")),
        ),
        out_specs=(
            P(None, None, ("ctx", "head")),
            P(None, None, ("ctx", "head")),
            P(None, None, ("ctx", "head")),
        ),
        check_vma=False,
    )
```

```python
import functools
import math

import jax
import jax.numpy as jnp
from jax import lax
from jax.experimental import pallas as pl
from jax.experimental.pallas import tpu as pltpu
from jax.sharding import PartitionSpec as P

CHUNKS = (8, 8)
PER_STEP = 4
GROUP = 4
MARK_ROWS = 16
VMEM = 32 * 1024 * 1024
PACK_VMEM = 56 * 1024 * 1024
LOG2E = 1.4426950408889634
HIDDEN = -1e30


def dot_tn(a, b):
    return lax.dot_general(a, b, (((0,), (0,)), ((), ())), preferred_element_type=jnp.float32)


def dot_nt(a, b):
    return lax.dot_general(a, b, (((1,), (1,)), ((), ())), preferred_element_type=jnp.float32)


def dot_nn(a, b):
    return lax.dot_general(a, b, (((1,), (0,)), ((), ())), preferred_element_type=jnp.float32)


def pack_kernel(first_ref, parity_ref, start_ref, k_ref, v_ref, q_ref, *rest, begin, rows):
    outs, sems = rest[:-1], rest[-1]
    half = start_ref.shape[1]
    parity = parity_ref[0]
    pieces = []
    for n, ref in enumerate((k_ref, v_ref, q_ref)):
        into = pl.ds(n * rows, rows)
        for core in range(2):
            source = ref.at[core, pl.ds(begin, rows)]
            pieces.append((source, outs[0].at[core, into]))
        for turn, out in enumerate(outs[1:]):
            if n < 2 or turn < 2:
                source = ref.at[lax.rem(parity + turn, 2), pl.ds(begin, rows)]
                pieces.append((source, out.at[0, into]))
    copies = [
        pltpu.make_async_copy(source, target, sems.at[i])
        for i, (source, target) in enumerate(pieces)
    ]
    for copy in copies:
        copy.start()
    into = first_ref[0] + lax.broadcasted_iota(jnp.int32, (1, half), 1) - start_ref[...]
    row = lax.broadcasted_iota(jnp.int32, (MARK_ROWS, half), 0)
    marks = jnp.where(row == 0, into // 2, jnp.where(row == 1, into % 2, 0))
    marks = marks.astype(jnp.float32).astype(jnp.bfloat16)
    for out in outs[:3]:
        for lead in range(out.shape[0]):
            out[lead, pl.ds(3 * rows, MARK_ROWS), :] = marks
    for copy in copies:
        copy.wait()


def pack(first, parity, starts, keys, values, queries, begin, chunk, direct):
    _, _, depth, half = keys.shape
    rows = chunk * depth
    flat = [x.reshape(2, -1, half) for x in (keys, values, queries)]
    whole, pair = 3 * rows + MARK_ROWS, 2 * rows
    out = [(2, whole, half), (1, whole, half), (1, whole, half), (1, pair, half), (1, pair, half)]
    out = [jax.ShapeDtypeStruct(shape, jnp.bfloat16) for shape in (out if direct else out[:1])]
    smem = pl.BlockSpec(memory_space=pltpu.SMEM)
    vmem = pl.BlockSpec(memory_space=pltpu.VMEM)
    return pl.pallas_call(
        functools.partial(pack_kernel, begin=begin * depth, rows=rows),
        in_specs=[smem, smem, vmem] + [pl.BlockSpec(memory_space=pltpu.HBM)] * 3,
        out_specs=[vmem] * len(out),
        out_shape=out,
        scratch_shapes=[pltpu.SemaphoreType.DMA((16,))],
        compiler_params=pltpu.CompilerParams(vmem_limit_bytes=PACK_VMEM),
        name="pack",
    )(first, parity, starts, *flat)


def attention_kernel(
    edge_ref, turned_ref, out_turn_ref, *refs, score_scale, parted
):
    next_marks, own_marks = refs[:2], refs[2]
    next_refs = (refs[3:6], refs[6:9])
    own_refs, prior_refs = refs[9:12], (refs[12:14], refs[14:16])
    results = refs[16:]
    if parted:
        to_next, kept, to_prior = results[:2], results[2:4], results[4:]
    else:
        to_next, kept, to_prior = ((ref.at[0], ref.at[1]) for ref in results)
    heads, _, depth, half = to_prior[0].shape
    span = 2 * half
    prior, own, following = range(3)
    outs = (to_prior, kept, to_next)
    turned = turned_ref[0]
    turns = (turned, 0, turned)
    out_turn = out_turn_ref[0]

    def positions(b, axis):
        shape = (1, span) if axis == 1 else (span, span)
        return lax.broadcasted_iota(jnp.int32, shape, axis) ^ (turns[b] * half)

    def first_visible(b, before):
        first, second = next_marks if b == following else (own_marks.at[0], own_marks.at[1])
        first, second = (first[0], second[0]) if b == following else (first[...], second[...])
        marks = jnp.concatenate([first, second], axis=1).astype(jnp.float32)
        into = (marks[0:1] * 2 + marks[1:2]).astype(jnp.int32)
        return before * span + positions(b, 1) - into

    def load(b, h, n):
        rows = pl.ds(h * depth, depth)
        if b == own:
            first, second = own_refs[n][0, rows, :], own_refs[n][1, rows, :]
        else:
            first, second = (prior_refs, None, next_refs)[b]
            first, second = first[n][0, rows, :], second[n][0, rows, :]
        return jnp.concatenate([first, second], axis=1)

    def put(b, pair, index, value, add):
        straight = (turns[b] ^ out_turn) == 0
        first, second = value[:, :half], value[:, half:]
        parts = (jnp.where(straight, first, second), jnp.where(straight, second, first))
        for ref, part in zip(pair, parts):
            if add:
                part = part + ref[index].astype(jnp.float32)
            ref[index] = part.astype(ref.dtype)

    def run(blocks, lo, rows_out, add=None):
        diagonal = len(blocks) - 1
        hidden = []
        for at in range(len(blocks)):
            key_pos = positions(blocks[at], 0) + at * span
            visible = key_pos >= lo
            if at == diagonal:
                visible = visible & (key_pos <= positions(blocks[at], 1) + at * span)
            hidden.append(jnp.where(visible, 0.0, HIDDEN))
        ones = jnp.ones((MARK_ROWS, span), jnp.bfloat16)
        for begin in range(0, heads, GROUP):
            group = range(begin, begin + GROUP)
            keys = {h: [load(b, h, 0) for b in blocks] for h in group}
            values = {h: [load(b, h, 1) for b in blocks] for h in group}
            q = {h: load(blocks[-1], h, 2) for h in group}
            scores = {
                h: [
                    dot_tn(key, q[h]) * (score_scale * LOG2E) + mask
                    for key, mask in zip(keys[h], hidden)
                ]
                for h in group
            }
            peak = {
                h: functools.reduce(
                    jnp.maximum, [jnp.max(score, axis=0, keepdims=True) for score in scores[h]]
                )
                for h in group
            }
            wide = {h: [jnp.exp2(score - peak[h]) for score in scores[h]] for h in group}
            low = {h: [weight.astype(jnp.bfloat16) for weight in wide[h]] for h in group}
            raw = {
                h: sum(
                    dot_nn(jnp.concatenate([value, ones], axis=0), weight)
                    for value, weight in zip(values[h], low[h])
                )
                for h in group
            }
            shared, row_dot = {}, {}
            for h in group:
                inverse = 1.0 / raw[h][depth : depth + 1]
                attended = (raw[h][:depth] * inverse).astype(jnp.bfloat16).astype(jnp.float32)
                row_dot[h] = jnp.sum(attended * attended, axis=0, keepdims=True) * inverse
                shared[h] = (attended * inverse).astype(jnp.bfloat16)
            grad_values = {h: [dot_nt(shared[h], weight) for weight in low[h]] for h in group}
            grad_scores = {
                h: [
                    (weight * (dot_tn(value, shared[h]) - row_dot[h])).astype(jnp.bfloat16)
                    for value, weight in zip(values[h], wide[h])
                ]
                for h in group
            }
            dq = {
                h: sum(dot_nn(key, grad) for key, grad in zip(keys[h], grad_scores[h]))
                for h in group
            }
            grad_keys = {h: [dot_nt(q[h], grad) for grad in grad_scores[h]] for h in group}
            for h in group:
                for at, b in enumerate(blocks):
                    put(b, outs[b], (h, 1), grad_values[h][at], b == add)
                    put(b, outs[b], (h, 0), grad_keys[h][at] * score_scale, b == add)
                put(blocks[-1], rows_out, (h, 2), dq[h] * score_scale, False)

    def clear(pair, kinds):
        for ref in pair:
            for n in kinds:
                ref[:, n] = jnp.zeros_like(ref[:, n])

    edge = edge_ref[0] == 1

    @pl.when(jnp.logical_not(edge))
    def _():
        lo = first_visible(following, 2)
        far = jnp.min(lo) < span
        clear(kept, (2,))

        @pl.when(far)
        def _():
            run((prior, own, following), lo, to_next)

        @pl.when(jnp.logical_not(far))
        def _():
            run((own, following), lo - span, to_next)
            clear(to_prior, (0, 1))

    @pl.when(edge)
    def _():
        lo_own = first_visible(own, 1)
        lo_next = first_visible(following, 1)
        across_own = jnp.min(lo_own) < span
        across_next = jnp.min(lo_next) < span

        @pl.when(across_own)
        def _():
            run((prior, own), lo_own, kept)

        @pl.when(jnp.logical_not(across_own))
        def _():
            run((own,), lo_own - span, kept)
            clear(to_prior, (0, 1))

        @pl.when(across_next)
        def _():
            run((own, following), lo_next, to_next, add=own)

        @pl.when(jnp.logical_not(across_next))
        def _():
            run((following,), lo_next - span, to_next)


def attention(edge, turned, out_turn, following, own, prior, score_scale, depth, parted):
    _, rows, half = own.shape
    chunk = rows // 3 // depth
    steps = chunk // PER_STEP
    block = PER_STEP * depth

    def spec(kinds):
        if parted:
            return [pl.BlockSpec((PER_STEP, kinds, depth, half), lambda g, e, t, o: (g, 0, 0, 0))] * 2
        return [pl.BlockSpec((2, PER_STEP, kinds, depth, half), lambda g, e, t, o: (0, g, 0, 0, 0))]

    def out(kinds):
        if parted:
            return [jax.ShapeDtypeStruct((chunk, kinds, depth, half), jnp.bfloat16)] * 2
        return [jax.ShapeDtypeStruct((2, chunk, kinds, depth, half), jnp.bfloat16)]

    def side(lead, n, cores=1):
        return pl.BlockSpec((cores, block, half), lambda g, e, t, o: (lead, n * steps + g, 0))

    def marks(lead, cores=1):
        return pl.BlockSpec(
            (cores, MARK_ROWS, half), lambda g, e, t, o: (lead, 3 * chunk * depth // MARK_ROWS, 0)
        )

    (first, first_row), (second, second_row) = following
    (prior0, prior0_row), (prior1, prior1_row) = prior
    specs = [marks(first_row), marks(second_row), marks(0, 2)]
    specs += [side(first_row, n) for n in range(3)] + [side(second_row, n) for n in range(3)]
    specs += [side(0, n, 2) for n in range(3)]
    for row in (prior0_row, prior1_row):
        specs += [side(row, n) for n in range(2)]
    pairs = chunk * (2 * half) * (6 * half)
    return pl.pallas_call(
        functools.partial(attention_kernel, score_scale=score_scale, parted=parted),
        grid_spec=pltpu.PrefetchScalarGridSpec(
            num_scalar_prefetch=3,
            grid=(steps,),
            in_specs=specs,
            out_specs=spec(3) + spec(3) + spec(2),
        ),
        out_shape=out(3) + out(3) + out(2),
        compiler_params=pltpu.CompilerParams(vmem_limit_bytes=PACK_VMEM),
        cost_estimate=pl.CostEstimate(
            flops=pairs * depth * 12, bytes_accessed=chunk * depth * half * 40, transcendentals=pairs
        ),
        name="attention",
    )(
        edge, turned, out_turn, first, second, own, *[first] * 3, *[second] * 3, *[own] * 3,
        *[prior0] * 2, *[prior1] * 2,
    )


def merge_kernel(kept_ref, from_prior_ref, *rest):
    *from_next_refs, out_ref = rest
    for n in range(3):
        total = kept_ref[:, :, n].astype(jnp.float32) + from_prior_ref[:, :, n].astype(jnp.float32)
        if n < 2:
            for ref in from_next_refs:
                total = total + ref[:, :, n].astype(jnp.float32)
        out_ref[:, :, n] = total.astype(jnp.bfloat16)


def merge(kept, from_prior, *from_next):
    _, chunk, _, depth, half = kept.shape

    def spec(kinds):
        return pl.BlockSpec((2, PER_STEP, kinds, depth, half), lambda g: (0, g, 0, 0, 0))

    return pl.pallas_call(
        merge_kernel,
        grid=(chunk // PER_STEP,),
        in_specs=[spec(3), spec(3)] + [spec(2)] * len(from_next),
        out_specs=spec(3),
        out_shape=jax.ShapeDtypeStruct(kept.shape, jnp.bfloat16),
        compiler_params=pltpu.CompilerParams(vmem_limit_bytes=PACK_VMEM),
        name="merge",
    )(kept, from_prior, *from_next)


def place_kernel(early_ref, out_q, out_k, out_v, sems):
    pieces = []
    for half in range(2):
        for n, out in enumerate((out_k, out_v, out_q)):
            pieces.append((early_ref.at[half, :, n], out.at[half, pl.ds(0, early_ref.shape[1])]))
    copies = [
        pltpu.make_async_copy(source, target, sems.at[i])
        for i, (source, target) in enumerate(pieces)
    ]
    for copy in copies:
        copy.start()
    for copy in copies:
        copy.wait()


def place(early, mine):
    _, _, _, depth, half = early.shape
    return pl.pallas_call(
        place_kernel,
        in_specs=[pl.BlockSpec(memory_space=pltpu.VMEM)],
        out_specs=[pl.BlockSpec(memory_space=pl.ANY)] * 3,
        out_shape=[jax.ShapeDtypeStruct((2, mine, depth, half), jnp.bfloat16)] * 3,
        scratch_shapes=[pltpu.SemaphoreType.DMA((6,))],
        compiler_params=pltpu.CompilerParams(vmem_limit_bytes=VMEM),
        name="place",
    )(early)


def finish_kernel(head_half_ref, kept_ref, from_prior_ref, from_next_ref, *refs):
    out_q, out_k, out_v = refs[3:]
    for n, out in enumerate((out_k, out_v, out_q)):
        total = kept_ref[:, n].astype(jnp.float32) + from_prior_ref[:, n].astype(jnp.float32)
        if n < 2:
            total = total + from_next_ref[:, n].astype(jnp.float32)
        out[0] = total.astype(jnp.bfloat16)


def finish(head_half, kept, from_prior, from_next, grads):
    chunk, _, depth, half = kept.shape
    before = (grads[0].shape[1] - chunk) // PER_STEP

    def spec(kinds):
        return pl.BlockSpec((PER_STEP, kinds, depth, half), lambda g, p: (g, 0, 0, 0))

    into = pl.BlockSpec((1, PER_STEP, depth, half), lambda g, p: (p[0], before + g, 0, 0))
    return pl.pallas_call(
        finish_kernel,
        grid_spec=pltpu.PrefetchScalarGridSpec(
            num_scalar_prefetch=1,
            grid=(chunk // PER_STEP,),
            in_specs=[spec(3), spec(3), spec(2)] + [pl.BlockSpec(memory_space=pl.ANY)] * 3,
            out_specs=[into] * 3,
        ),
        out_shape=[jax.ShapeDtypeStruct(x.shape, x.dtype) for x in grads],
        input_output_aliases={4: 0, 5: 1, 6: 2},
        compiler_params=pltpu.CompilerParams(vmem_limit_bytes=PACK_VMEM),
        name="finish",
    )(head_half, kept, from_prior, from_next, *grads)


def after(value, *earlier):
    return lax.optimization_barrier((value, *earlier))[0]


def shards(queries, keys, values, doc_start):
    heads, depth, half = queries.shape
    score_scale = 1.0 / math.sqrt(depth)
    ctx_count = lax.axis_size("ctx")
    head_count = lax.axis_size("head")
    mine = heads // 2
    pairs = [[2 * z, 2 * z + 1] for z in range(head_count // 2)]

    def cores(value):
        return lax.all_to_all(
            value, "head", split_axis=0, concat_axis=0, tiled=True, axis_index_groups=pairs
        )

    column_up = [
        (c * head_count + s, c * head_count + s + 2)
        for c in range(ctx_count)
        for s in range(head_count - 2)
    ]
    across = [
        (c * head_count - 2 + core, c * head_count + core)
        for c in range(1, ctx_count)
        for core in range(2)
    ]
    inner_up = [
        (c * head_count + s, c * head_count + s + 2)
        for c in range(ctx_count)
        for s in range(2, head_count - 4)
    ]
    column_down = [(t, s) for s, t in column_up]
    inner_down = [(t, s) for s, t in inner_up]
    across_down = [(t, s) for s, t in across]
    flat = ("ctx", "head")
    begins = (0, CHUNKS[0])
    by_core = (2, mine, depth, half)
    keys, values, queries = (x.reshape(by_core) for x in (keys, values, queries))
    position = (lax.axis_index("ctx") * head_count + lax.axis_index("head")) * half
    first = position.astype(jnp.int32).reshape(1)
    starts = doc_start.reshape(1, half)

    parity = (lax.axis_index("head") % 2).astype(jnp.int32).reshape(1)
    edge = (lax.axis_index("head") < 2).astype(jnp.int32).reshape(1)

    def packed(c):
        return pack(first, parity, starts, keys, values, queries, begins[c], CHUNKS[c], c == 0)

    own, following, prior, to_next, kept, to_prior, back_next, back_prior, done = (
        [None, None] for _ in range(9)
    )
    crossed_down = [(t, s ^ 1) for s, t in column_up]
    by_halves, same, crossed, same_pair, crossed_pair = packed(0)
    same = lax.ppermute(same, flat, column_down)
    crossed = lax.ppermute(crossed, flat, crossed_down)
    following[0] = ((same, 0), (crossed, 0))
    same_pair = lax.ppermute(same_pair, flat, inner_up + across)
    crossed_pair = lax.ppermute(crossed_pair, flat, [(s, t ^ 1) for s, t in inner_up + across])
    prior[0] = ((same_pair, 0), (crossed_pair, 0))
    own[1] = cores(packed(1)[0])
    own[0] = cores(after(by_halves, own[1]))
    gone = lax.ppermute(after(own[1][:, : 2 * CHUNKS[1] * depth], same), flat, inner_up + across)
    prior[1] = ((gone, 0), (gone, 1))
    came = lax.ppermute(after(own[1], same, crossed, own[0], same_pair, crossed_pair), flat, column_down)
    following[1] = ((came, 0), (came, 1))

    nothing = jnp.zeros_like(parity)
    to_next[0], kept[0], to_prior[0] = attention(
        edge, parity, nothing, following[0], own[0], prior[0], score_scale, depth, False,
    )
    far_end = lax.ppermute(to_prior[0], flat, across_down)
    back_next[0] = lax.ppermute(after(to_next[0], gone), flat, column_up)
    back_prior[0] = lax.ppermute(after(to_prior[0], came, far_end), flat, inner_down)
    next_same, next_crossed, kept_same, kept_crossed, prior_same, prior_crossed = attention(
        edge, nothing, parity, following[1], own[1], prior[1], score_scale, depth, True
    )
    crossed_column = [(s, t ^ 1) for s, t in column_up]
    down = inner_down + across_down
    next_same = lax.ppermute(after(next_same, back_next[0]), flat, column_up)
    next_crossed = lax.ppermute(after(next_crossed, back_next[0]), flat, crossed_column)
    prior_same = lax.ppermute(after(prior_same, back_prior[0]), flat, down)
    prior_crossed = lax.ppermute(
        after(prior_crossed, back_prior[0]), flat, [(s, t ^ 1) for s, t in down]
    )
    kept_crossed = lax.ppermute(kept_crossed, "head", [(s, s ^ 1) for s in range(head_count)])
    early = cores(merge(kept[0], back_next[0], back_prior[0], far_end))
    grads = place(early, mine)
    grads = finish(parity, kept_same, next_same, prior_same, grads)
    grads = finish(1 - parity, kept_crossed, next_crossed, prior_crossed, grads)
    return tuple(x.reshape(heads, depth, half) for x in grads)


def solution(mesh):
    return jax.shard_map(
        shards,
        mesh=mesh,
        in_specs=(
            P(None, None, ("ctx", "head")),
            P(None, None, ("ctx", "head")),
            P(None, None, ("ctx", "head")),
            P(("ctx", "head")),
        ),
        out_specs=(
            P(None, None, ("ctx", "head")),
            P(None, None, ("ctx", "head")),
            P(None, None, ("ctx", "head")),
        ),
        check_vma=False,
    )
```

```python
import functools
import math

import jax
import jax.numpy as jnp
from jax import lax
from jax.experimental import pallas as pl
from jax.experimental.pallas import tpu as pltpu
from jax.sharding import PartitionSpec as P

CHUNKS = (8, 8)
PER_STEP = 4
GROUP = 4
MARK_ROWS = 16
VMEM = 32 * 1024 * 1024
PACK_VMEM = 56 * 1024 * 1024
LOG2E = 1.4426950408889634
HIDDEN = -1e30


def dot_tn(a, b):
    return lax.dot_general(a, b, (((0,), (0,)), ((), ())), preferred_element_type=jnp.float32)


def dot_nt(a, b):
    return lax.dot_general(a, b, (((1,), (1,)), ((), ())), preferred_element_type=jnp.float32)


def dot_nn(a, b):
    return lax.dot_general(a, b, (((1,), (0,)), ((), ())), preferred_element_type=jnp.float32)


def pack_kernel(first_ref, parity_ref, start_ref, k_ref, v_ref, q_ref, *rest, begin, rows, whole, pairs):
    outs, sems = rest[:-1], rest[-1]
    half = start_ref.shape[1]
    parity = parity_ref[0]
    pieces = []
    for n, ref in enumerate((k_ref, v_ref, q_ref)):
        into = pl.ds(n * rows, rows)
        if whole:
            for core in range(2):
                pieces.append((ref.at[core, pl.ds(begin, rows)], outs[0].at[core, into]))
        else:
            for turn, out in enumerate(outs if n < 2 else outs[:2]):
                source = ref.at[lax.rem(parity + turn, 2), pl.ds(begin, rows)]
                pieces.append((source, out.at[0, into]))
    copies = [
        pltpu.make_async_copy(source, target, sems.at[i])
        for i, (source, target) in enumerate(pieces)
    ]
    for copy in copies:
        copy.start()
    into = first_ref[0] + lax.broadcasted_iota(jnp.int32, (1, half), 1) - start_ref[...]
    row = lax.broadcasted_iota(jnp.int32, (MARK_ROWS, half), 0)
    marks = jnp.where(row == 0, into // 2, jnp.where(row == 1, into % 2, 0))
    marks = marks.astype(jnp.float32).astype(jnp.bfloat16)
    for out in outs[: 1 if whole else 2]:
        for lead in range(out.shape[0]):
            out[lead, pl.ds(3 * rows, MARK_ROWS), :] = marks
    for copy in copies:
        copy.wait()


def pack(first, parity, starts, keys, values, queries, begin, chunk, whole, pairs):
    _, _, depth, half = keys.shape
    rows = chunk * depth
    flat = [x.reshape(2, -1, half) for x in (keys, values, queries)]
    full = 3 * rows + MARK_ROWS
    shapes = [(2, full, half)] if whole else [(1, full, half)] * 2
    shapes += [(1, 2 * rows, half)] * (2 * pairs)
    smem = pl.BlockSpec(memory_space=pltpu.SMEM)
    vmem = pl.BlockSpec(memory_space=pltpu.VMEM)
    return pl.pallas_call(
        functools.partial(pack_kernel, begin=begin * depth, rows=rows, whole=whole, pairs=pairs),
        in_specs=[smem, smem, vmem] + [pl.BlockSpec(memory_space=pltpu.HBM)] * 3,
        out_specs=[vmem] * len(shapes),
        out_shape=[jax.ShapeDtypeStruct(shape, jnp.bfloat16) for shape in shapes],
        scratch_shapes=[pltpu.SemaphoreType.DMA((10,))],
        compiler_params=pltpu.CompilerParams(vmem_limit_bytes=PACK_VMEM),
        name="pack",
    )(first, parity, starts, *flat)


def attention_kernel(
    edge_ref, turned_ref, out_turn_ref, *refs, score_scale, parted
):
    next_marks, own_marks = refs[:2], refs[2:4]
    next_refs, own_refs = (refs[4:7], refs[7:10]), (refs[10:13], refs[13:16])
    prior_refs, results = (refs[16:18], refs[18:20]), refs[20:]
    if parted:
        to_next, kept, to_prior = results[:2], results[2:4], results[4:]
    else:
        to_next, kept, to_prior = ((ref.at[0], ref.at[1]) for ref in results)
    heads, _, depth, half = to_prior[0].shape
    span = 2 * half
    prior, own, following = range(3)
    outs = (to_prior, kept, to_next)
    turned = turned_ref[0]
    out_turn = out_turn_ref[0]

    def positions(axis):
        shape = (1, span) if axis == 1 else (span, span)
        return lax.broadcasted_iota(jnp.int32, shape, axis) ^ (turned * half)

    def first_visible(b, before):
        first, second = next_marks if b == following else own_marks
        marks = jnp.concatenate([first[0], second[0]], axis=1).astype(jnp.float32)
        into = (marks[0:1] * 2 + marks[1:2]).astype(jnp.int32)
        return before * span + positions(1) - into

    def load(b, h, n):
        rows = pl.ds(h * depth, depth)
        first, second = (prior_refs, own_refs, next_refs)[b]
        return jnp.concatenate([first[n][0, rows, :], second[n][0, rows, :]], axis=1)

    def put(pair, index, value, add):
        straight = (turned ^ out_turn) == 0
        first, second = value[:, :half], value[:, half:]
        parts = (jnp.where(straight, first, second), jnp.where(straight, second, first))
        for ref, part in zip(pair, parts):
            if add:
                part = part + ref[index].astype(jnp.float32)
            ref[index] = part.astype(ref.dtype)

    def run(blocks, lo, rows_out, add=None):
        diagonal = len(blocks) - 1
        hidden = []
        for at in range(len(blocks)):
            key_pos = positions(0) + at * span
            visible = key_pos >= lo
            if at == diagonal:
                visible = visible & (key_pos <= positions(1) + at * span)
            hidden.append(jnp.where(visible, 0.0, HIDDEN))
        ones = jnp.ones((MARK_ROWS, span), jnp.bfloat16)
        for begin in range(0, heads, GROUP):
            group = range(begin, begin + GROUP)
            keys = {h: [load(b, h, 0) for b in blocks] for h in group}
            values = {h: [load(b, h, 1) for b in blocks] for h in group}
            q = {h: load(blocks[-1], h, 2) for h in group}
            scores = {
                h: [
                    dot_tn(key, q[h]) * (score_scale * LOG2E) + mask
                    for key, mask in zip(keys[h], hidden)
                ]
                for h in group
            }
            peak = {
                h: functools.reduce(
                    jnp.maximum, [jnp.max(score, axis=0, keepdims=True) for score in scores[h]]
                )
                for h in group
            }
            wide = {h: [jnp.exp2(score - peak[h]) for score in scores[h]] for h in group}
            low = {h: [weight.astype(jnp.bfloat16) for weight in wide[h]] for h in group}
            raw = {
                h: sum(
                    dot_nn(jnp.concatenate([value, ones], axis=0), weight)
                    for value, weight in zip(values[h], low[h])
                )
                for h in group
            }
            shared, row_dot = {}, {}
            for h in group:
                inverse = 1.0 / raw[h][depth : depth + 1]
                attended = (raw[h][:depth] * inverse).astype(jnp.bfloat16).astype(jnp.float32)
                row_dot[h] = jnp.sum(attended * attended, axis=0, keepdims=True) * inverse
                shared[h] = (attended * inverse).astype(jnp.bfloat16)
            grad_values = {h: [dot_nt(shared[h], weight) for weight in low[h]] for h in group}
            grad_scores = {
                h: [
                    (weight * (dot_tn(value, shared[h]) - row_dot[h])).astype(jnp.bfloat16)
                    for value, weight in zip(values[h], wide[h])
                ]
                for h in group
            }
            dq = {
                h: sum(dot_nn(key, grad) for key, grad in zip(keys[h], grad_scores[h]))
                for h in group
            }
            grad_keys = {h: [dot_nt(q[h], grad) for grad in grad_scores[h]] for h in group}
            for h in group:
                for at, b in enumerate(blocks):
                    put(outs[b], (h, 1), grad_values[h][at], b == add)
                    put(outs[b], (h, 0), grad_keys[h][at] * score_scale, b == add)
                put(rows_out, (h, 2), dq[h] * score_scale, False)

    def clear(pair, kinds):
        for ref in pair:
            for n in kinds:
                ref[:, n] = jnp.zeros_like(ref[:, n])

    edge = edge_ref[0] == 1

    @pl.when(jnp.logical_not(edge))
    def _():
        lo = first_visible(following, 2)
        far = jnp.min(lo) < span
        clear(kept, (2,))

        @pl.when(far)
        def _():
            run((prior, own, following), lo, to_next)

        @pl.when(jnp.logical_not(far))
        def _():
            run((own, following), lo - span, to_next)
            clear(to_prior, (0, 1))

    @pl.when(edge)
    def _():
        lo_own = first_visible(own, 1)
        lo_next = first_visible(following, 1)
        across_own = jnp.min(lo_own) < span
        across_next = jnp.min(lo_next) < span

        @pl.when(across_own)
        def _():
            run((prior, own), lo_own, kept)

        @pl.when(jnp.logical_not(across_own))
        def _():
            run((own,), lo_own - span, kept)
            clear(to_prior, (0, 1))

        @pl.when(across_next)
        def _():
            run((own, following), lo_next, to_next, add=own)

        @pl.when(jnp.logical_not(across_next))
        def _():
            run((following,), lo_next - span, to_next)


def attention(edge, turned, out_turn, following, own, prior, score_scale, depth, parted):
    (first, first_row), (second, second_row) = following
    (own0, own0_row), (own1, own1_row) = own
    _, rows, half = own0.shape
    chunk = rows // 3 // depth
    steps = chunk // PER_STEP
    block = PER_STEP * depth

    def spec(kinds):
        if parted:
            return [pl.BlockSpec((PER_STEP, kinds, depth, half), lambda g, e, t, o: (g, 0, 0, 0))] * 2
        return [pl.BlockSpec((2, PER_STEP, kinds, depth, half), lambda g, e, t, o: (0, g, 0, 0, 0))]

    def out(kinds):
        if parted:
            return [jax.ShapeDtypeStruct((chunk, kinds, depth, half), jnp.bfloat16)] * 2
        return [jax.ShapeDtypeStruct((2, chunk, kinds, depth, half), jnp.bfloat16)]

    def side(lead, n):
        return pl.BlockSpec((1, block, half), lambda g, e, t, o: (lead, n * steps + g, 0))

    def marks(lead):
        return pl.BlockSpec(
            (1, MARK_ROWS, half), lambda g, e, t, o: (lead, 3 * chunk * depth // MARK_ROWS, 0)
        )

    (prior0, prior0_row), (prior1, prior1_row) = prior
    own_and_next = (first_row, second_row, own0_row, own1_row)
    specs = [marks(row) for row in own_and_next]
    for row in own_and_next:
        specs += [side(row, n) for n in range(3)]
    for row in (prior0_row, prior1_row):
        specs += [side(row, n) for n in range(2)]
    pairs = chunk * (2 * half) * (6 * half)
    return pl.pallas_call(
        functools.partial(attention_kernel, score_scale=score_scale, parted=parted),
        grid_spec=pltpu.PrefetchScalarGridSpec(
            num_scalar_prefetch=3,
            grid=(steps,),
            in_specs=specs,
            out_specs=spec(3) + spec(3) + spec(2),
        ),
        out_shape=out(3) + out(3) + out(2),
        compiler_params=pltpu.CompilerParams(vmem_limit_bytes=PACK_VMEM),
        cost_estimate=pl.CostEstimate(
            flops=pairs * depth * 12, bytes_accessed=chunk * depth * half * 40, transcendentals=pairs
        ),
        name="attention",
    )(
        edge, turned, out_turn, first, second, own0, own1, *[first] * 3, *[second] * 3,
        *[own0] * 3, *[own1] * 3, *[prior0] * 2, *[prior1] * 2,
    )


def merge_kernel(kept_ref, from_prior_ref, *rest):
    *from_next_refs, out_ref = rest
    for n in range(3):
        total = kept_ref[:, :, n].astype(jnp.float32) + from_prior_ref[:, :, n].astype(jnp.float32)
        if n < 2:
            for ref in from_next_refs:
                total = total + ref[:, :, n].astype(jnp.float32)
        out_ref[:, :, n] = total.astype(jnp.bfloat16)


def merge(kept, from_prior, *from_next):
    _, chunk, _, depth, half = kept.shape

    def spec(kinds):
        return pl.BlockSpec((2, PER_STEP, kinds, depth, half), lambda g: (0, g, 0, 0, 0))

    return pl.pallas_call(
        merge_kernel,
        grid=(chunk // PER_STEP,),
        in_specs=[spec(3), spec(3)] + [spec(2)] * len(from_next),
        out_specs=spec(3),
        out_shape=jax.ShapeDtypeStruct(kept.shape, jnp.bfloat16),
        compiler_params=pltpu.CompilerParams(vmem_limit_bytes=PACK_VMEM),
        name="merge",
    )(kept, from_prior, *from_next)


def place_kernel(early_ref, out_q, out_k, out_v, sems):
    pieces = []
    for half in range(2):
        for n, out in enumerate((out_k, out_v, out_q)):
            pieces.append((early_ref.at[half, :, n], out.at[half, pl.ds(0, early_ref.shape[1])]))
    copies = [
        pltpu.make_async_copy(source, target, sems.at[i])
        for i, (source, target) in enumerate(pieces)
    ]
    for copy in copies:
        copy.start()
    for copy in copies:
        copy.wait()


def place(early, mine):
    _, _, _, depth, half = early.shape
    return pl.pallas_call(
        place_kernel,
        in_specs=[pl.BlockSpec(memory_space=pltpu.VMEM)],
        out_specs=[pl.BlockSpec(memory_space=pl.ANY)] * 3,
        out_shape=[jax.ShapeDtypeStruct((2, mine, depth, half), jnp.bfloat16)] * 3,
        scratch_shapes=[pltpu.SemaphoreType.DMA((6,))],
        compiler_params=pltpu.CompilerParams(vmem_limit_bytes=VMEM),
        name="place",
    )(early)


def finish_kernel(head_half_ref, kept_ref, from_prior_ref, from_next_ref, *refs):
    out_q, out_k, out_v = refs[3:]
    for n, out in enumerate((out_k, out_v, out_q)):
        total = kept_ref[:, n].astype(jnp.float32) + from_prior_ref[:, n].astype(jnp.float32)
        if n < 2:
            total = total + from_next_ref[:, n].astype(jnp.float32)
        out[0] = total.astype(jnp.bfloat16)


def finish(head_half, kept, from_prior, from_next, grads):
    chunk, _, depth, half = kept.shape
    before = (grads[0].shape[1] - chunk) // PER_STEP

    def spec(kinds):
        return pl.BlockSpec((PER_STEP, kinds, depth, half), lambda g, p: (g, 0, 0, 0))

    into = pl.BlockSpec((1, PER_STEP, depth, half), lambda g, p: (p[0], before + g, 0, 0))
    return pl.pallas_call(
        finish_kernel,
        grid_spec=pltpu.PrefetchScalarGridSpec(
            num_scalar_prefetch=1,
            grid=(chunk // PER_STEP,),
            in_specs=[spec(3), spec(3), spec(2)] + [pl.BlockSpec(memory_space=pl.ANY)] * 3,
            out_specs=[into] * 3,
        ),
        out_shape=[jax.ShapeDtypeStruct(x.shape, x.dtype) for x in grads],
        input_output_aliases={4: 0, 5: 1, 6: 2},
        compiler_params=pltpu.CompilerParams(vmem_limit_bytes=PACK_VMEM),
        name="finish",
    )(head_half, kept, from_prior, from_next, *grads)


def after(value, *earlier):
    return lax.optimization_barrier((value, *earlier))[0]


def shards(queries, keys, values, doc_start):
    heads, depth, half = queries.shape
    score_scale = 1.0 / math.sqrt(depth)
    ctx_count = lax.axis_size("ctx")
    head_count = lax.axis_size("head")
    mine = heads // 2
    pairs = [[2 * z, 2 * z + 1] for z in range(head_count // 2)]

    def cores(value):
        return lax.all_to_all(
            value, "head", split_axis=0, concat_axis=0, tiled=True, axis_index_groups=pairs
        )

    column_up = [
        (c * head_count + s, c * head_count + s + 2)
        for c in range(ctx_count)
        for s in range(head_count - 2)
    ]
    across = [
        (c * head_count - 2 + core, c * head_count + core)
        for c in range(1, ctx_count)
        for core in range(2)
    ]
    inner_up = [
        (c * head_count + s, c * head_count + s + 2)
        for c in range(ctx_count)
        for s in range(2, head_count - 4)
    ]
    column_down = [(t, s) for s, t in column_up]
    inner_down = [(t, s) for s, t in inner_up]
    across_down = [(t, s) for s, t in across]
    flat = ("ctx", "head")
    begins = (0, CHUNKS[0])
    by_core = (2, mine, depth, half)
    keys, values, queries = (x.reshape(by_core) for x in (keys, values, queries))
    position = (lax.axis_index("ctx") * head_count + lax.axis_index("head")) * half
    first = position.astype(jnp.int32).reshape(1)
    starts = doc_start.reshape(1, half)

    parity = (lax.axis_index("head") % 2).astype(jnp.int32).reshape(1)
    edge = (lax.axis_index("head") < 2).astype(jnp.int32).reshape(1)

    def packed(c, whole, pairs, *earlier):
        marked = after(starts, *earlier) if earlier else starts
        return pack(
            first, parity, marked, keys, values, queries, begins[c], CHUNKS[c], whole, pairs
        )

    own, following, prior, to_next, kept, to_prior, back_next, back_prior, done = (
        [None, None] for _ in range(9)
    )
    crossed_down = [(t, s ^ 1) for s, t in column_up]
    same, crossed, same_pair, crossed_pair = packed(0, 0, 1)
    swapped = lax.ppermute(crossed, "head", [(s, s ^ 1) for s in range(head_count)])
    own[0] = ((same, 0), (swapped, 0))
    same = lax.ppermute(same, flat, column_down)
    crossed = lax.ppermute(crossed, flat, crossed_down)
    following[0] = ((same, 0), (crossed, 0))
    same_pair = lax.ppermute(same_pair, flat, inner_up + across)
    crossed_pair = lax.ppermute(crossed_pair, flat, [(s, t ^ 1) for s, t in inner_up + across])
    prior[0] = ((same_pair, 0), (crossed_pair, 0))
    whole = cores(packed(1, 1, 0)[0])
    own[1] = ((whole, 0), (whole, 1))
    gone = lax.ppermute(after(whole[:, : 2 * CHUNKS[1] * depth], same), flat, inner_up + across)
    prior[1] = ((gone, 0), (gone, 1))
    came = lax.ppermute(after(whole, same, crossed, same_pair, crossed_pair), flat, column_down)
    following[1] = ((came, 0), (came, 1))

    nothing = jnp.zeros_like(parity)
    to_next[0], kept[0], to_prior[0] = attention(
        edge, parity, nothing, following[0], own[0], prior[0], score_scale, depth, False,
    )
    far_end = lax.ppermute(to_prior[0], flat, across_down)
    back_next[0] = lax.ppermute(after(to_next[0], gone), flat, column_up)
    back_prior[0] = lax.ppermute(after(to_prior[0], came, far_end), flat, inner_down)
    next_same, next_crossed, kept_same, kept_crossed, prior_same, prior_crossed = attention(
        edge, nothing, parity, following[1], own[1], prior[1], score_scale, depth, True
    )
    crossed_column = [(s, t ^ 1) for s, t in column_up]
    down = inner_down + across_down
    next_same = lax.ppermute(next_same, flat, column_up)
    next_crossed = lax.ppermute(after(next_crossed, back_next[0]), flat, crossed_column)
    prior_same = lax.ppermute(after(prior_same, back_prior[0]), flat, down)
    prior_crossed = lax.ppermute(
        after(prior_crossed, back_prior[0]), flat, [(s, t ^ 1) for s, t in down]
    )
    kept_crossed = lax.ppermute(kept_crossed, "head", [(s, s ^ 1) for s in range(head_count)])
    early = cores(merge(kept[0], back_next[0], back_prior[0], far_end))
    grads = place(early, mine)
    grads = finish(parity, kept_same, next_same, prior_same, grads)
    grads = finish(1 - parity, kept_crossed, next_crossed, prior_crossed, grads)
    return tuple(x.reshape(heads, depth, half) for x in grads)


def solution(mesh):
    return jax.shard_map(
        shards,
        mesh=mesh,
        in_specs=(
            P(None, None, ("ctx", "head")),
            P(None, None, ("ctx", "head")),
            P(None, None, ("ctx", "head")),
            P(("ctx", "head")),
        ),
        out_specs=(
            P(None, None, ("ctx", "head")),
            P(None, None, ("ctx", "head")),
            P(None, None, ("ctx", "head")),
        ),
        check_vma=False,
    )
```

```python
import functools
import math

import jax
import jax.numpy as jnp
from jax import lax
from jax.experimental import pallas as pl
from jax.experimental.pallas import tpu as pltpu
from jax.sharding import PartitionSpec as P

CHUNKS = (8, 8)
PER_STEP = 4
GROUP = 4
MARK_ROWS = 16
VMEM = 32 * 1024 * 1024
PACK_VMEM = 56 * 1024 * 1024
LOG2E = 1.4426950408889634
HIDDEN = -1e30


def dot_tn(a, b):
    return lax.dot_general(a, b, (((0,), (0,)), ((), ())), preferred_element_type=jnp.float32)


def dot_nt(a, b):
    return lax.dot_general(a, b, (((1,), (1,)), ((), ())), preferred_element_type=jnp.float32)


def dot_nn(a, b):
    return lax.dot_general(a, b, (((1,), (0,)), ((), ())), preferred_element_type=jnp.float32)


def pack_kernel(first_ref, parity_ref, start_ref, k_ref, v_ref, q_ref, *rest, begin, rows, whole, pairs):
    outs, sems = rest[:-1], rest[-1]
    half = start_ref.shape[1]
    parity = parity_ref[0]
    pieces = []
    for n, ref in enumerate((k_ref, v_ref, q_ref)):
        into = pl.ds(n * rows, rows)
        if whole:
            for core in range(2):
                pieces.append((ref.at[core, pl.ds(begin, rows)], outs[0].at[core, into]))
        else:
            for turn, out in enumerate(outs if n < 2 else outs[:2]):
                source = ref.at[lax.rem(parity + turn, 2), pl.ds(begin, rows)]
                pieces.append((source, out.at[0, into]))
    copies = [
        pltpu.make_async_copy(source, target, sems.at[i])
        for i, (source, target) in enumerate(pieces)
    ]
    for copy in copies:
        copy.start()
    into = first_ref[0] + lax.broadcasted_iota(jnp.int32, (1, half), 1) - start_ref[...]
    row = lax.broadcasted_iota(jnp.int32, (MARK_ROWS, half), 0)
    marks = jnp.where(row == 0, into // 2, jnp.where(row == 1, into % 2, 0))
    marks = marks.astype(jnp.float32).astype(jnp.bfloat16)
    for out in outs[: 1 if whole else 2]:
        for lead in range(out.shape[0]):
            out[lead, pl.ds(3 * rows, MARK_ROWS), :] = marks
    for copy in copies:
        copy.wait()


def pack(first, parity, starts, keys, values, queries, begin, chunk, whole, pairs):
    _, _, depth, half = keys.shape
    rows = chunk * depth
    flat = [x.reshape(2, -1, half) for x in (keys, values, queries)]
    full = 3 * rows + MARK_ROWS
    shapes = [(2, full, half)] if whole else [(1, full, half)] * 2
    shapes += [(1, 2 * rows, half)] * (2 * pairs)
    smem = pl.BlockSpec(memory_space=pltpu.SMEM)
    vmem = pl.BlockSpec(memory_space=pltpu.VMEM)
    return pl.pallas_call(
        functools.partial(pack_kernel, begin=begin * depth, rows=rows, whole=whole, pairs=pairs),
        in_specs=[smem, smem, vmem] + [pl.BlockSpec(memory_space=pltpu.HBM)] * 3,
        out_specs=[vmem] * len(shapes),
        out_shape=[jax.ShapeDtypeStruct(shape, jnp.bfloat16) for shape in shapes],
        scratch_shapes=[pltpu.SemaphoreType.DMA((10,))],
        compiler_params=pltpu.CompilerParams(vmem_limit_bytes=PACK_VMEM),
        name="pack",
    )(first, parity, starts, *flat)


def attention_kernel(
    edge_ref, turned_ref, out_turn_ref, *refs, score_scale, parted
):
    next_marks, own_marks = refs[:2], refs[2:4]
    next_refs, own_refs = (refs[4:7], refs[7:10]), (refs[10:13], refs[13:16])
    prior_refs, results = (refs[16:18], refs[18:20]), refs[20:]
    if parted:
        to_next, kept, to_prior = results[:2], results[2:4], results[4:]
    else:
        to_next, kept, to_prior = ((ref.at[0], ref.at[1]) for ref in results)
    heads, _, depth, half = to_prior[0].shape
    span = 2 * half
    prior, own, following = range(3)
    outs = (to_prior, kept, to_next)
    turned = turned_ref[0]
    out_turn = out_turn_ref[0]

    def positions(axis):
        shape = (1, span) if axis == 1 else (span, span)
        return lax.broadcasted_iota(jnp.int32, shape, axis) ^ (turned * half)

    def first_visible(b, before):
        first, second = next_marks if b == following else own_marks
        marks = jnp.concatenate([first[0], second[0]], axis=1).astype(jnp.float32)
        into = (marks[0:1] * 2 + marks[1:2]).astype(jnp.int32)
        return before * span + positions(1) - into

    def load(b, h, n):
        rows = pl.ds(h * depth, depth)
        first, second = (prior_refs, own_refs, next_refs)[b]
        return jnp.concatenate([first[n][0, rows, :], second[n][0, rows, :]], axis=1)

    def put(pair, index, value, add):
        straight = (turned ^ out_turn) == 0
        first, second = value[:, :half], value[:, half:]
        parts = (jnp.where(straight, first, second), jnp.where(straight, second, first))
        for ref, part in zip(pair, parts):
            if add:
                part = part + ref[index].astype(jnp.float32)
            ref[index] = part.astype(ref.dtype)

    def run(blocks, lo, rows_out, add=None):
        diagonal = len(blocks) - 1
        hidden = []
        for at in range(len(blocks)):
            key_pos = positions(0) + at * span
            visible = key_pos >= lo
            if at == diagonal:
                visible = visible & (key_pos <= positions(1) + at * span)
            hidden.append(jnp.where(visible, 0.0, HIDDEN))
        ones = jnp.ones((MARK_ROWS, span), jnp.bfloat16)
        for begin in range(0, heads, GROUP):
            group = range(begin, begin + GROUP)
            keys = {h: [load(b, h, 0) for b in blocks] for h in group}
            values = {h: [load(b, h, 1) for b in blocks] for h in group}
            q = {h: load(blocks[-1], h, 2) for h in group}
            scores = {
                h: [
                    dot_tn(key, q[h]) * (score_scale * LOG2E) + mask
                    for key, mask in zip(keys[h], hidden)
                ]
                for h in group
            }
            peak = {
                h: functools.reduce(
                    jnp.maximum, [jnp.max(score, axis=0, keepdims=True) for score in scores[h]]
                )
                for h in group
            }
            wide = {h: [jnp.exp2(score - peak[h]) for score in scores[h]] for h in group}
            low = {h: [weight.astype(jnp.bfloat16) for weight in wide[h]] for h in group}
            raw = {
                h: sum(
                    dot_nn(jnp.concatenate([value, ones], axis=0), weight)
                    for value, weight in zip(values[h], low[h])
                )
                for h in group
            }
            shared, row_dot = {}, {}
            for h in group:
                inverse = 1.0 / raw[h][depth : depth + 1]
                attended = (raw[h][:depth] * inverse).astype(jnp.bfloat16).astype(jnp.float32)
                row_dot[h] = jnp.sum(attended * attended, axis=0, keepdims=True) * inverse
                shared[h] = (attended * inverse).astype(jnp.bfloat16)
            grad_values = {h: [dot_nt(shared[h], weight) for weight in low[h]] for h in group}
            grad_scores = {
                h: [
                    (weight * (dot_tn(value, shared[h]) - row_dot[h])).astype(jnp.bfloat16)
                    for value, weight in zip(values[h], wide[h])
                ]
                for h in group
            }
            dq = {
                h: sum(dot_nn(key, grad) for key, grad in zip(keys[h], grad_scores[h]))
                for h in group
            }
            grad_keys = {h: [dot_nt(q[h], grad) for grad in grad_scores[h]] for h in group}
            for h in group:
                for at, b in enumerate(blocks):
                    put(outs[b], (h, 1), grad_values[h][at], b == add)
                    put(outs[b], (h, 0), grad_keys[h][at] * score_scale, b == add)
                put(rows_out, (h, 2), dq[h] * score_scale, False)

    def clear(pair, kinds):
        for ref in pair:
            for n in kinds:
                ref[:, n] = jnp.zeros_like(ref[:, n])

    edge = edge_ref[0] == 1

    @pl.when(jnp.logical_not(edge))
    def _():
        lo = first_visible(following, 2)
        far = jnp.min(lo) < span
        clear(kept, (2,))

        @pl.when(far)
        def _():
            run((prior, own, following), lo, to_next)

        @pl.when(jnp.logical_not(far))
        def _():
            run((own, following), lo - span, to_next)
            clear(to_prior, (0, 1))

    @pl.when(edge)
    def _():
        lo_own = first_visible(own, 1)
        lo_next = first_visible(following, 1)
        across_own = jnp.min(lo_own) < span
        across_next = jnp.min(lo_next) < span

        @pl.when(across_own)
        def _():
            run((prior, own), lo_own, kept)

        @pl.when(jnp.logical_not(across_own))
        def _():
            run((own,), lo_own - span, kept)
            clear(to_prior, (0, 1))

        @pl.when(across_next)
        def _():
            run((own, following), lo_next, to_next, add=own)

        @pl.when(jnp.logical_not(across_next))
        def _():
            run((following,), lo_next - span, to_next)


def attention(edge, turned, out_turn, following, own, prior, score_scale, depth, parted):
    (first, first_row), (second, second_row) = following
    (own0, own0_row), (own1, own1_row) = own
    _, rows, half = own0.shape
    chunk = rows // 3 // depth
    steps = chunk // PER_STEP
    block = PER_STEP * depth

    def spec(kinds):
        if parted:
            return [pl.BlockSpec((PER_STEP, kinds, depth, half), lambda g, e, t, o: (g, 0, 0, 0))] * 2
        return [pl.BlockSpec((2, PER_STEP, kinds, depth, half), lambda g, e, t, o: (0, g, 0, 0, 0))]

    def out(kinds):
        if parted:
            return [jax.ShapeDtypeStruct((chunk, kinds, depth, half), jnp.bfloat16)] * 2
        return [jax.ShapeDtypeStruct((2, chunk, kinds, depth, half), jnp.bfloat16)]

    def side(lead, n):
        return pl.BlockSpec((1, block, half), lambda g, e, t, o: (lead, n * steps + g, 0))

    def marks(lead):
        return pl.BlockSpec(
            (1, MARK_ROWS, half), lambda g, e, t, o: (lead, 3 * chunk * depth // MARK_ROWS, 0)
        )

    (prior0, prior0_row), (prior1, prior1_row) = prior
    own_and_next = (first_row, second_row, own0_row, own1_row)
    specs = [marks(row) for row in own_and_next]
    for row in own_and_next:
        specs += [side(row, n) for n in range(3)]
    for row in (prior0_row, prior1_row):
        specs += [side(row, n) for n in range(2)]
    pairs = chunk * (2 * half) * (6 * half)
    return pl.pallas_call(
        functools.partial(attention_kernel, score_scale=score_scale, parted=parted),
        grid_spec=pltpu.PrefetchScalarGridSpec(
            num_scalar_prefetch=3,
            grid=(steps,),
            in_specs=specs,
            out_specs=spec(3) + spec(3) + spec(2),
        ),
        out_shape=out(3) + out(3) + out(2),
        compiler_params=pltpu.CompilerParams(vmem_limit_bytes=PACK_VMEM),
        cost_estimate=pl.CostEstimate(
            flops=pairs * depth * 12, bytes_accessed=chunk * depth * half * 40, transcendentals=pairs
        ),
        name="attention",
    )(
        edge, turned, out_turn, first, second, own0, own1, *[first] * 3, *[second] * 3,
        *[own0] * 3, *[own1] * 3, *[prior0] * 2, *[prior1] * 2,
    )


def merge_kernel(kept_ref, from_prior_ref, *rest):
    *from_next_refs, out_ref = rest
    for n in range(3):
        total = kept_ref[:, :, n].astype(jnp.float32) + from_prior_ref[:, :, n].astype(jnp.float32)
        if n < 2:
            for ref in from_next_refs:
                total = total + ref[:, :, n].astype(jnp.float32)
        out_ref[:, :, n] = total.astype(jnp.bfloat16)


def merge(kept, from_prior, *from_next):
    _, chunk, _, depth, half = kept.shape

    def spec(kinds):
        return pl.BlockSpec((2, PER_STEP, kinds, depth, half), lambda g: (0, g, 0, 0, 0))

    return pl.pallas_call(
        merge_kernel,
        grid=(chunk // PER_STEP,),
        in_specs=[spec(3), spec(3)] + [spec(2)] * len(from_next),
        out_specs=spec(3),
        out_shape=jax.ShapeDtypeStruct(kept.shape, jnp.bfloat16),
        compiler_params=pltpu.CompilerParams(vmem_limit_bytes=PACK_VMEM),
        name="merge",
    )(kept, from_prior, *from_next)


def place_kernel(early_ref, out_q, out_k, out_v, sems):
    pieces = []
    for half in range(2):
        for n, out in enumerate((out_k, out_v, out_q)):
            pieces.append((early_ref.at[half, :, n], out.at[half, pl.ds(0, early_ref.shape[1])]))
    copies = [
        pltpu.make_async_copy(source, target, sems.at[i])
        for i, (source, target) in enumerate(pieces)
    ]
    for copy in copies:
        copy.start()
    for copy in copies:
        copy.wait()


def place(early, mine):
    _, _, _, depth, half = early.shape
    return pl.pallas_call(
        place_kernel,
        in_specs=[pl.BlockSpec(memory_space=pltpu.VMEM)],
        out_specs=[pl.BlockSpec(memory_space=pl.ANY)] * 3,
        out_shape=[jax.ShapeDtypeStruct((2, mine, depth, half), jnp.bfloat16)] * 3,
        scratch_shapes=[pltpu.SemaphoreType.DMA((6,))],
        compiler_params=pltpu.CompilerParams(vmem_limit_bytes=VMEM),
        name="place",
    )(early)


def finish_kernel(head_half_ref, kept_ref, from_prior_ref, from_next_ref, *refs):
    out_q, out_k, out_v = refs[3:]
    for n, out in enumerate((out_k, out_v, out_q)):
        total = kept_ref[:, n].astype(jnp.float32) + from_prior_ref[:, n].astype(jnp.float32)
        if n < 2:
            total = total + from_next_ref[:, n].astype(jnp.float32)
        out[0] = total.astype(jnp.bfloat16)


def finish(head_half, kept, from_prior, from_next, grads):
    chunk, _, depth, half = kept.shape
    before = (grads[0].shape[1] - chunk) // PER_STEP

    def spec(kinds):
        return pl.BlockSpec((PER_STEP, kinds, depth, half), lambda g, p: (g, 0, 0, 0))

    into = pl.BlockSpec((1, PER_STEP, depth, half), lambda g, p: (p[0], before + g, 0, 0))
    return pl.pallas_call(
        finish_kernel,
        grid_spec=pltpu.PrefetchScalarGridSpec(
            num_scalar_prefetch=1,
            grid=(chunk // PER_STEP,),
            in_specs=[spec(3), spec(3), spec(2)] + [pl.BlockSpec(memory_space=pl.ANY)] * 3,
            out_specs=[into] * 3,
        ),
        out_shape=[jax.ShapeDtypeStruct(x.shape, x.dtype) for x in grads],
        input_output_aliases={4: 0, 5: 1, 6: 2},
        compiler_params=pltpu.CompilerParams(vmem_limit_bytes=PACK_VMEM),
        name="finish",
    )(head_half, kept, from_prior, from_next, *grads)


def after(value, *earlier):
    return lax.optimization_barrier((value, *earlier))[0]


def shards(queries, keys, values, doc_start):
    heads, depth, half = queries.shape
    score_scale = 1.0 / math.sqrt(depth)
    ctx_count = lax.axis_size("ctx")
    head_count = lax.axis_size("head")
    mine = heads // 2
    pairs = [[2 * z, 2 * z + 1] for z in range(head_count // 2)]

    def cores(value):
        return lax.all_to_all(
            value, "head", split_axis=0, concat_axis=0, tiled=True, axis_index_groups=pairs
        )

    column_up = [
        (c * head_count + s, c * head_count + s + 2)
        for c in range(ctx_count)
        for s in range(head_count - 2)
    ]
    across = [
        (c * head_count - 2 + core, c * head_count + core)
        for c in range(1, ctx_count)
        for core in range(2)
    ]
    inner_up = [
        (c * head_count + s, c * head_count + s + 2)
        for c in range(ctx_count)
        for s in range(2, head_count - 4)
    ]
    column_down = [(t, s) for s, t in column_up]
    inner_down = [(t, s) for s, t in inner_up]
    across_down = [(t, s) for s, t in across]
    flat = ("ctx", "head")
    begins = (0, CHUNKS[0])
    by_core = (2, mine, depth, half)
    keys, values, queries = (x.reshape(by_core) for x in (keys, values, queries))
    position = (lax.axis_index("ctx") * head_count + lax.axis_index("head")) * half
    first = position.astype(jnp.int32).reshape(1)
    starts = doc_start.reshape(1, half)

    parity = (lax.axis_index("head") % 2).astype(jnp.int32).reshape(1)
    edge = (lax.axis_index("head") < 2).astype(jnp.int32).reshape(1)

    def packed(c, whole, pairs, *earlier):
        marked = after(starts, *earlier) if earlier else starts
        return pack(
            first, parity, marked, keys, values, queries, begins[c], CHUNKS[c], whole, pairs
        )

    own, following, prior, to_next, kept, to_prior, back_next, back_prior, done = (
        [None, None] for _ in range(9)
    )
    crossed_down = [(t, s ^ 1) for s, t in column_up]
    same, crossed, same_pair, crossed_pair = packed(0, 0, 1)
    swapped = lax.ppermute(crossed, "head", [(s, s ^ 1) for s in range(head_count)])
    own[0] = ((same, 0), (swapped, 0))
    same = lax.ppermute(same, flat, column_down)
    crossed = lax.ppermute(crossed, flat, crossed_down)
    following[0] = ((same, 0), (crossed, 0))
    same_pair = lax.ppermute(same_pair, flat, inner_up + across)
    crossed_pair = lax.ppermute(crossed_pair, flat, [(s, t ^ 1) for s, t in inner_up + across])
    prior[0] = ((same_pair, 0), (crossed_pair, 0))
    whole = cores(packed(1, 1, 0)[0])
    own[1] = ((whole, 0), (whole, 1))
    gone = lax.ppermute(after(whole[:, : 2 * CHUNKS[1] * depth], same), flat, inner_up + across)
    prior[1] = ((gone, 0), (gone, 1))
    came = lax.ppermute(after(whole, same, crossed, same_pair, crossed_pair), flat, column_down)
    following[1] = ((came, 0), (came, 1))

    nothing = jnp.zeros_like(parity)
    to_next[0], kept[0], to_prior[0] = attention(
        edge, parity, nothing, following[0], own[0], prior[0], score_scale, depth, False,
    )
    far_end = lax.ppermute(to_prior[0], flat, across_down)
    back_next[0] = lax.ppermute(after(to_next[0], gone), flat, column_up)
    back_prior[0] = lax.ppermute(after(to_prior[0], came), flat, inner_down)
    next_same, next_crossed, kept_same, kept_crossed, prior_same, prior_crossed = attention(
        edge, nothing, parity, following[1], own[1], prior[1], score_scale, depth, True
    )
    crossed_column = [(s, t ^ 1) for s, t in column_up]
    down = inner_down + across_down
    next_same = lax.ppermute(next_same, flat, column_up)
    next_crossed = lax.ppermute(after(next_crossed, back_next[0], far_end), flat, crossed_column)
    prior_same = lax.ppermute(after(prior_same, back_prior[0]), flat, down)
    prior_crossed = lax.ppermute(
        after(prior_crossed, back_prior[0]), flat, [(s, t ^ 1) for s, t in down]
    )
    kept_crossed = lax.ppermute(kept_crossed, "head", [(s, s ^ 1) for s in range(head_count)])
    early = cores(merge(kept[0], back_next[0], back_prior[0], far_end))
    grads = place(early, mine)
    grads = finish(parity, kept_same, next_same, prior_same, grads)
    grads = finish(1 - parity, kept_crossed, next_crossed, prior_crossed, grads)
    return tuple(x.reshape(heads, depth, half) for x in grads)


def solution(mesh):
    return jax.shard_map(
        shards,
        mesh=mesh,
        in_specs=(
            P(None, None, ("ctx", "head")),
            P(None, None, ("ctx", "head")),
            P(None, None, ("ctx", "head")),
            P(("ctx", "head")),
        ),
        out_specs=(
            P(None, None, ("ctx", "head")),
            P(None, None, ("ctx", "head")),
            P(None, None, ("ctx", "head")),
        ),
        check_vma=False,
    )
```
